32 devices in a mesh: groups: 2 (over y), dp: 4 (over x, core), tensor: 4 (over z).
Axes of the slice: x: 2, y: 2, z: 4, core: 2. Of those that a mesh axis runs over, the one named last changes fastest.
Arguments:
- hidden: bfloat16 [8192, 8192], P(('groups', 'dp'), 'tensor'), parts along dimension 0, may hold values from -6 to 6
- key_value_weight: bfloat16 [8192, 2048], P('tensor'), may hold values from -0.0625 to 0.0625
- adapter_down_factors: bfloat16 [8192, 512], P('tensor', 'dp'), may hold values from -0.0625 to 0.0625
- adapter_up_factors: bfloat16 [512, 2048], P('dp', 'tensor'), may hold values from -0.75 to 0.75
- row_adapter: int32 [8192, 1], P(('groups', 'dp')), parts along dimension 0, may hold values from 0 to 7; in each aligned block of 1024 rows (0 to 1023, 1024 to 2047, ...) at most 256 rows name the same one
- rank_of_adapter: int32 [8], replicated, may hold values from 16 to 64
- adapter_storage_slot: int32 [8], replicated, may hold values from 0 to 7, each once
Outputs:
- projected: bfloat16 [8192, 2048], P(('groups', 'dp'), 'tensor'), parts along dimension 0
The draws below stay inside these ranges and needn't reach their ends.
There are 2 independent parts, one for each index of `groups`. The reference program is written for one: setup_inputs(seed, part) draws one part's arguments, and reference() takes and returns one part's arrays. A program takes and returns all parts, laid end to end along the dimension named above; an argument that names none is the same for every part. Nothing has to cross between parts.
Inputs may be any that keep to these rules, and one draw needn't show every extreme that they name: `row_adapter`: in the rows of one index of dp no adapter is named more than 256 times, a bound that some block reaches. `adapter_storage_slot`: each slot holds one adapter.
All inputs are finite; a program needn't handle non-finite values.
Results may differ from the reference program's by a relative error of at most 0.013.
Values may be sent and summed in bfloat16 or wider, within the bound.
No kernel may reach another device: no remote copies, remote signals or barrier semaphores. Data moves between devices by JAX's collectives and lax.ppermute only.
A program may use at most 128 MiB of HBM per device.

```python
import math
import jax
import jax.numpy as jnp
import numpy as np
from jax import lax

MODEL_WIDTH = 8192
KEY_VALUE_COLUMNS = 2048
LARGEST_RANK = 64
ROWS_DEV = 1024
ADAPTER_COUNT = 8
CAP = 256
TOKENS = 4096
N_TENSOR = 4


def plant(result, key, least, largest):
    dims = result.shape
    spot = [jax.random.randint(jax.random.fold_in(key, axis), (), 0, dims[axis]) for axis in range(len(dims))]
    result = result.at[tuple(spot)].set(least)
    longest = dims.index(max(dims))
    spot[longest] = (spot[longest] + 1) % dims[longest]
    return result.at[tuple(spot)].set(largest)


def block_scale(rng, dims, split, smallest, largest):
    def one(axis_at, blocks):
        draws = jax.random.uniform(jax.random.fold_in(jax.random.fold_in(rng, 6), axis_at), (blocks,), jnp.float32, smallest / len(split), largest / len(split))
        return jnp.repeat(jnp.exp(draws), dims[axis_at] // blocks).reshape((-1,) + (1,) * (len(dims) - axis_at - 1))

    loudness = one(*split[0])
    for cut in split[1:]:
        loudness = loudness * one(*cut)
    return loudness


def assign_block(key, own, number, rows, number_of, top, bound, skew):
    sequence = jax.random.permutation(key, number_of)
    packed, ordinary = load_shares(number_of, rows * top, bound, skew, True), load_shares(number_of, rows * top, bound, skew, False)
    places = jnp.arange(number_of)

    def named(lengths, rotation):
        used = int((lengths > 0).sum())
        fixed = max(1, used // 4)
        passed = fixed + (places - fixed + rotation * (used - fixed)) % max(1, number_of - fixed)
        return jnp.zeros((number_of,), jnp.int32).at[sequence[jnp.where(places < fixed, places, passed)]].set(jnp.asarray(lengths, jnp.int32))

    lengths = jnp.where(number % 4 == 0, named(packed, number // 4), named(ordinary, number - number // 4 - 1))
    mixed = jax.random.permutation(jax.random.fold_in(own, 3), number_of)
    donor, taker = mixed[0:number_of // 2 * 2:2], mixed[1:number_of // 2 * 2:2]
    room = jnp.minimum(lengths[donor] - 1, bound - lengths[taker]) // 2
    room = jnp.where((donor == sequence[0]) | (taker == sequence[0]) | (lengths[taker] == 0), 0, jnp.maximum(room, 0))
    passed = jax.random.randint(jax.random.fold_in(own, 4), (number_of // 2,), 0, 1 << 20) % (room + 1)
    lengths = lengths.at[donor].add(-passed).at[taker].add(passed)
    members = jnp.searchsorted(jnp.cumsum(lengths), jnp.arange(rows * top), side="right").astype(jnp.int32)
    grid = members.reshape(top, rows).T
    grid = grid[jax.random.permutation(jax.random.fold_in(own, 1), rows)]
    rotation = jax.random.randint(jax.random.fold_in(own, 2), (rows, 1), 0, top)
    return jnp.take_along_axis(grid, (jnp.arange(top)[None, :] + rotation) % top, axis=1)


def load_shares(number_of, total, most, slope, full):
    loads = [(1 << 20) // math.isqrt(rank ** slope) + 1 for rank in range(1, number_of + 1)]
    largest = most if full else min(most, max(-(-total // number_of), total * loads[0] // sum(loads)))
    least = 1 if total - largest >= number_of - 1 else 0
    given, surplus = [largest] + [least] * (number_of - 1), total - largest - least * (number_of - 1)
    while surplus > 0:
        candidates = [i for i in range(1, number_of) if given[i] < largest] or [i for i in range(1, number_of) if given[i] < most]
        whole, left = sum([loads[i] for i in candidates]), surplus
        for i in candidates:
            addition = min(most - given[i], max(1, left * loads[i] // whole), surplus)
            given[i] = given[i] + addition
            surplus = surplus - addition
    return np.array(given)


def scatter_about(own_key, extent, deviation, most, split=(), kind=jnp.bfloat16):
    array = deviation * jax.random.normal(own_key, extent, jnp.float32)
    if split:
        array = array * block_scale(own_key, extent, split, -0.22, 0.18)
    return jnp.clip(array, -most, most).astype(kind)


def setup_inputs(seed: int = 0, part: int = 0) -> dict:
    keys = jax.random.split(jax.random.key(seed), 8)
    own_keys = jax.random.split(jax.random.fold_in(keys[7], part), 8)
    hidden = scatter_about(own_keys[0], (TOKENS, MODEL_WIDTH), 1.0, 6.0, ((0, 4), (1, 4)))
    key_value_weight = scatter_about(keys[1], (MODEL_WIDTH, KEY_VALUE_COLUMNS), MODEL_WIDTH ** -0.5, 0.0625, ((0, 4),))
    adapter_down_factors = scatter_about(keys[2], (MODEL_WIDTH, ADAPTER_COUNT * LARGEST_RANK), MODEL_WIDTH ** -0.5, 0.0625, ((0, 4), (1, 4)))
    adapter_up_factors = scatter_about(keys[3], (ADAPTER_COUNT * LARGEST_RANK, KEY_VALUE_COLUMNS), LARGEST_RANK ** -0.5, 0.75, ((0, 4), (1, 4)))
    row_adapter_keys = jax.random.split(jax.random.fold_in(own_keys[4], 1), TOKENS // ROWS_DEV)
    row_adapter_turns = jax.random.permutation(jax.random.fold_in(own_keys[4], 3), TOKENS // ROWS_DEV)
    row_adapter = jax.vmap(lambda own, number: assign_block(jax.random.fold_in(own_keys[4], 2), own, number, ROWS_DEV, ADAPTER_COUNT, 1, CAP, 2))(row_adapter_keys, row_adapter_turns).reshape((TOKENS, 1))
    rank_of_adapter = plant(jax.random.randint(keys[5], (ADAPTER_COUNT,), LARGEST_RANK // 4, LARGEST_RANK + 1), jax.random.fold_in(keys[5], 1), LARGEST_RANK // 4, LARGEST_RANK).astype(jnp.int32)
    adapter_storage_slot = jax.random.permutation(keys[6], ADAPTER_COUNT).astype(jnp.int32)
    return {"hidden": hidden, "key_value_weight": key_value_weight, "adapter_down_factors": adapter_down_factors, "adapter_up_factors": adapter_up_factors, "row_adapter": row_adapter, "rank_of_adapter": rank_of_adapter, "adapter_storage_slot": adapter_storage_slot}


def reference(hidden, key_value_weight, adapter_down_factors, adapter_up_factors, row_adapter, rank_of_adapter, adapter_storage_slot):
    shard_width = MODEL_WIDTH // N_TENSOR

    def add_block(index, running):
        x_block = lax.dynamic_slice_in_dim(hidden, index * shard_width, shard_width, 1)
        w_block = lax.dynamic_slice_in_dim(key_value_weight, index * shard_width, shard_width, 0)
        rounded = jnp.dot(x_block, w_block, preferred_element_type=jnp.float32).astype(jnp.bfloat16)
        rounded = lax.optimization_barrier(rounded)
        return running + rounded.astype(jnp.float32)

    base_sum = lax.fori_loop(0, N_TENSOR, add_block, jnp.zeros((TOKENS, KEY_VALUE_COLUMNS), jnp.float32))
    row_ids = row_adapter[:, 0]
    slot_row = adapter_storage_slot[row_ids]
    rank_row = rank_of_adapter[row_ids]

    def down_step(running, storage_index):
        factor_matrix = lax.dynamic_slice_in_dim(adapter_down_factors, storage_index * LARGEST_RANK, LARGEST_RANK, 1)
        product = jnp.dot(hidden, factor_matrix, preferred_element_type=jnp.float32)
        return running + jnp.where((slot_row == storage_index)[:, None], product, jnp.float32(0.0)), None

    slots = jnp.arange(ADAPTER_COUNT, dtype=jnp.int32)
    low_full, _ = lax.scan(down_step, jnp.zeros((TOKENS, LARGEST_RANK), jnp.float32), slots)
    columns = jnp.arange(LARGEST_RANK, dtype=jnp.int32)
    live_cols = columns[None, :] < rank_row[:, None]
    scaling = LARGEST_RANK / (2.0 * rank_row.astype(jnp.float32))
    low_rank = jnp.where(live_cols, low_full * scaling[:, None], jnp.float32(0.0)).astype(jnp.bfloat16)

    def up_step(running, storage_index):
        factor_matrix = lax.dynamic_slice_in_dim(adapter_up_factors, storage_index * LARGEST_RANK, LARGEST_RANK, 0)
        product = jnp.dot(low_rank, factor_matrix, preferred_element_type=jnp.float32)
        return running + jnp.where((slot_row == storage_index)[:, None], product, jnp.float32(0.0)), None

    adapter_out, _ = lax.scan(up_step, jnp.zeros((TOKENS, KEY_VALUE_COLUMNS), jnp.float32), slots)
    return (base_sum + adapter_out).astype(jnp.bfloat16)
```

```python
import jax
import jax.numpy as jnp
from jax import lax
from jax.sharding import PartitionSpec as P

F32 = jnp.float32
BF16 = jnp.bfloat16


def gather_dp(block, axis, size):
    held = block
    bit = size // 2
    while bit:
        other = lax.ppermute(held, "dp", [(i, i ^ bit) for i in range(size)])
        held = (held, other, bit)
        bit //= 2
    return held


def line_of_four(
    hidden, weight, down, up, row_adapter, rank_of_adapter, adapter_storage_slot
):
    rows = hidden.shape[0]
    half = rows // 2
    cols = weight.shape[1] // 4
    dp = lax.axis_size("dp")
    adapters = rank_of_adapter.shape[0]
    width = down.shape[1] * dp // adapters
    per_dev = adapters // dp
    me = lax.axis_index("tensor")
    at = lax.axis_index("dp")

    table = jnp.array([[3, 2, 1, 0], [3, 2, 0, 1], [0, 1, 3, 2], [0, 1, 2, 3]], jnp.int32)

    def part(phase, lo, hi):
        block = lax.dynamic_slice_in_dim(weight, table[me, phase] * cols, cols, 1)
        return jnp.dot(hidden[lo:hi], block, preferred_element_type=F32)

    ends = [(0, 1), (3, 2)]
    middle = [(1, 2), (2, 1)]
    outward = [(2, 3), (1, 0)]

    def send(v, pairs):
        return lax.ppermute(v, "tensor", pairs)

    def add(a, b):
        return (a.astype(F32) + b.astype(F32)).astype(BF16)

    spans = [(0, half), (half, rows)]
    p0 = [part(0, *s).astype(BF16) for s in spans]
    a1 = [send(v, ends) for v in p0]

    def gather(block, axis):
        bit = dp // 2
        while bit:
            other = lax.ppermute(block, "dp", [(i, i ^ bit) for i in range(dp)])
            block = (block, other)
            block = jnp.concatenate(block, axis)
            bit //= 2
        return block

    place = [0]
    bit = dp // 2
    while bit:
        place = place + [p ^ bit for p in place]
        bit //= 2
    owner_at = jnp.array(place, jnp.int32) ^ at

    downs = gather(down, 1)
    ups = gather(up, 0)

    p1 = [part(1, *s).astype(BF16) for s in spans]
    a2 = [send(v, ends) for v in p1]
    b1 = [send(add(p, a), middle) for p, a in zip(p0, a1)]

    ids = row_adapter[:, 0]
    match = ids[:, None] == jnp.arange(adapters, dtype=jnp.int32)[None, :]
    slot = jnp.sum(jnp.where(match, adapter_storage_slot[None, :], 0), axis=1)
    rank = jnp.sum(jnp.where(match, rank_of_adapter[None, :], 0), axis=1)
    slot_at = (owner_at[:, None] * per_dev + jnp.arange(per_dev, dtype=jnp.int32)[None, :]).reshape(-1)
    chosen = slot[:, None] == slot_at[None, :]
    product = jnp.dot(hidden, downs, preferred_element_type=F32)
    low = jnp.einsum("rac,ra->rc", product.reshape(rows, adapters, width), chosen.astype(F32)).astype(BF16)
    e1 = send(low, ends)
    low = add(low, e1)
    e2 = send(low, middle)
    low = add(low, e2)
    e3 = send(low, outward)
    is_end = (me == 0) | (me == 3)
    low = jnp.where(is_end, e3, low).astype(F32)

    p2 = [part(2, *s).astype(BF16) for s in spans]
    a3 = [send(v, ends) for v in p2]
    b2 = [send(add(p, a), middle) for p, a in zip(p1, a2)]
    d1 = [send(add(p, a), outward) for p, a in zip(p2, b1)]

    live = jnp.arange(width, dtype=jnp.int32)[None, :] < rank[:, None]
    scaling = width / (2.0 * rank.astype(F32))
    low_rank = jnp.where(live, low * scaling[:, None], F32(0.0)).astype(BF16)
    spread = jnp.where(chosen[:, :, None], low_rank[:, None, :], jnp.zeros((), BF16)).reshape(rows, -1)
    out = []
    for k, s in enumerate(spans):
        own = part(3, *s) + jnp.dot(spread[s[0] : s[1]], ups, preferred_element_type=F32)
        total = own + b2[k].astype(F32) + d1[k].astype(F32)
        out.append((total + a3[k].astype(F32)).astype(BF16))
    return jnp.concatenate(out, 0)


def any_line(
    hidden, weight, down, up, row_adapter, rank_of_adapter, adapter_storage_slot
):
    rows = hidden.shape[0]
    adapters = rank_of_adapter.shape[0]
    width = down.shape[1] * lax.axis_size("dp") // adapters
    ids = row_adapter[:, 0]
    every = jnp.arange(adapters, dtype=jnp.int32)
    match = ids[:, None] == every[None, :]
    slot = jnp.sum(jnp.where(match, adapter_storage_slot[None, :], 0), axis=1)
    rank = jnp.sum(jnp.where(match, rank_of_adapter[None, :], 0), axis=1)
    chosen = slot[:, None] == every[None, :]
    partial = jnp.dot(hidden, weight, preferred_element_type=F32).astype(BF16)
    base = lax.psum_scatter(partial, "tensor", scatter_dimension=1, tiled=True).astype(F32)
    downs = lax.all_gather(down, "dp", axis=1, tiled=True)
    product = jnp.dot(hidden, downs, preferred_element_type=F32)
    low = jnp.einsum("rac,ra->rc", product.reshape(rows, adapters, width), chosen.astype(F32))
    low = lax.psum(low.astype(BF16), "tensor").astype(F32)
    live = jnp.arange(width, dtype=jnp.int32)[None, :] < rank[:, None]
    scaling = width / (2.0 * rank.astype(F32))
    low_rank = jnp.where(live, low * scaling[:, None], F32(0.0)).astype(BF16)
    spread = jnp.where(chosen[:, :, None], low_rank[:, None, :], jnp.zeros((), BF16)).reshape(rows, -1)
    ups = lax.all_gather(up, "dp", axis=0, tiled=True)
    return (base + jnp.dot(spread, ups, preferred_element_type=F32)).astype(BF16)


def solution(mesh):
    four = mesh.shape["tensor"] == 4 and mesh.shape["dp"] & (mesh.shape["dp"] - 1) == 0
    return jax.shard_map(
        line_of_four if four else any_line,
        mesh=mesh,
        in_specs=(
            P(("groups", "dp"), "tensor"),
            P("tensor", None),
            P("tensor", "dp"),
            P("dp", "tensor"),
            P(("groups", "dp"), None),
            P(),
            P(),
        ),
        out_specs=P(("groups", "dp"), "tensor"),
        check_vma=False,
    )
```

```python
import functools

import jax
import jax.numpy as jnp
from jax import lax
from jax.experimental import pallas as pl
from jax.experimental.pallas import tpu as pltpu
from jax.sharding import PartitionSpec as P

F32 = jnp.float32
BF16 = jnp.bfloat16
LANES = 128
PIECES = 4
ANY = pl.BlockSpec(memory_space=pl.ANY)
VMEM = pl.BlockSpec(memory_space=pltpu.VMEM)
PARAMS = pltpu.CompilerParams(vmem_limit_bytes=64 * 1024 * 1024 - 128 * 1024)
COST = pl.CostEstimate(flops=1, bytes_accessed=1, transcendentals=0)


def call(kernel, outs, in_specs, scratch, token, *args, out_specs, aliases=None):
    n_in, n_out = len(args), len(outs)
    aliases = dict(aliases or {})
    if token is not None:
        args += (token,)
        in_specs = [*in_specs, ANY]
        aliases[n_in] = n_out

    def body(*refs):
        given = refs[:n_in]
        rest = refs[len(args) :]
        kernel(*given, *rest[:n_out], *rest[n_out + 1 :])

    return pl.pallas_call(
        body,
        out_shape=(*outs, jax.ShapeDtypeStruct((8, LANES), F32)),
        in_specs=in_specs,
        out_specs=(*out_specs, ANY),
        scratch_shapes=scratch,
        input_output_aliases=aliases,
        compiler_params=PARAMS,
        cost_estimate=COST,
    )(*args)


def relay(token, *arrays):
    return call(
        lambda *refs: None,
        [jax.ShapeDtypeStruct(a.shape, a.dtype) for a in arrays],
        [ANY] * len(arrays),
        [],
        token,
        *arrays,
        out_specs=[ANY] * len(arrays),
        aliases={i: i for i in range(len(arrays))},
    )


def in_middle():
    me = lax.axis_index("tensor")
    return jnp.logical_and(me > 0, me < 3)


def block_of(phase):
    me = lax.axis_index("tensor")
    if phase == 0:
        return jnp.where(me < 2, 3, 0)
    if phase == 1:
        return jnp.where(me < 2, 2, 1)
    if phase == 2:
        return me + 1 - 2 * lax.rem(me, 2)
    return me


def copy_in(pairs, sems):
    copies = [pltpu.make_async_copy(a, b, sems.at[i]) for i, (a, b) in enumerate(pairs)]
    for c in copies:
        c.start()
    return copies


def fetch(hidden, weight, lo, rows, phase, h_buf, w_buf, h_sem, w_sem):
    depth, cols = w_buf.shape
    step = depth // PIECES
    first = pl.multiple_of(block_of(phase) * cols, cols)
    h_copies, w_copies = [], []
    for k in range(PIECES):
        span = pl.ds(k * step, step)
        if h_sem is not None:
            pair = (hidden.at[pl.ds(lo, rows), span], h_buf.at[pl.ds(lo, rows), span])
            h_copies += copy_in([pair], h_sem.at[pl.ds(k, 1)])
        pair = (weight.at[span, pl.ds(first, cols)], w_buf.at[span])
        w_copies += copy_in([pair], w_sem.at[pl.ds(k, 1)])
    return h_copies, w_copies


def product(h_buf, w_buf, lo, rows, copies):
    h_copies, w_copies = copies
    step = w_buf.shape[0] // PIECES
    total = None
    for k in range(PIECES):
        if h_copies:
            h_copies[k].wait()
        if w_copies:
            w_copies[k].wait()
        span = pl.ds(k * step, step)
        term = jnp.dot(h_buf[pl.ds(lo, rows), span], w_buf[span], preferred_element_type=F32)
        total = term if total is None else total + term
    return total


def first_kernel(rows, hidden, weight, out, h_buf, w_buf, h_sem, w_sem):
    copies = fetch(hidden, weight, 0, rows, 0, h_buf, w_buf, h_sem, w_sem)
    out[...] = product(h_buf, w_buf, 0, rows, copies).astype(BF16)


def first_product(hidden, weight, rows):
    depth, cols = hidden.shape[1], weight.shape[1] // 4
    return call(
        functools.partial(first_kernel, rows),
        [jax.ShapeDtypeStruct((rows, cols), BF16)],
        [ANY] * 2,
        [
            pltpu.VMEM((rows, depth), BF16),
            pltpu.VMEM((depth, cols), BF16),
            pltpu.SemaphoreType.DMA((PIECES,)),
            pltpu.SemaphoreType.DMA((PIECES,)),
        ],
        None,
        hidden,
        weight,
        out_specs=[VMEM],
    )


def next_kernel(start, hidden, weight, p0, p1a, p1b, p2, h_buf, w0, w1, w2, buf, h_sem, w_sem, o_sem):
    rows = hidden.shape[0]
    half = rows // 2
    copies0 = fetch(hidden, weight, start, rows - start, 0, h_buf, w0, h_sem.at[0], w_sem.at[0])
    if start:
        early = copy_in([(hidden.at[pl.ds(0, start)], h_buf.at[pl.ds(0, start)])], h_sem.at[1])
    copies1 = fetch(hidden, weight, 0, rows, 1, h_buf, w1, None, w_sem.at[1])
    copies2 = fetch(hidden, weight, 0, rows, 2, h_buf, w2, None, w_sem.at[2])
    buf[0, pl.ds(start, rows - start)] = product(h_buf, w0, start, rows - start, copies0).astype(BF16)
    outs = copy_in([(buf.at[0, pl.ds(start, rows - start)], p0)], o_sem.at[pl.ds(0, 1)])
    for c in early:
        c.wait()
    buf[1] = product(h_buf, w1, 0, rows, copies1).astype(BF16)
    outs += copy_in(
        [(buf.at[1, pl.ds(0, half)], p1a), (buf.at[1, pl.ds(half, half)], p1b)],
        o_sem.at[pl.ds(1, 2)],
    )
    buf[2] = product(h_buf, w2, 0, rows, copies2).astype(BF16)
    outs += copy_in([(buf.at[2], p2)], o_sem.at[pl.ds(3, 1)])
    for c in outs:
        c.wait()


def next_products(token, hidden, weight, start):
    rows, depth = hidden.shape
    cols = weight.shape[1] // 4
    shapes = [(rows - start, cols), (rows // 2, cols), (rows // 2, cols), (rows, cols)]
    return call(
        functools.partial(next_kernel, start),
        [jax.ShapeDtypeStruct(shape, BF16) for shape in shapes],
        [ANY] * 2,
        [
            pltpu.VMEM((rows, depth), BF16),
            pltpu.VMEM((depth, cols), BF16),
            pltpu.VMEM((depth, cols), BF16),
            pltpu.VMEM((depth, cols), BF16),
            pltpu.VMEM((3, rows, cols), BF16),
            pltpu.SemaphoreType.DMA((2, PIECES)),
            pltpu.SemaphoreType.DMA((3, PIECES)),
            pltpu.SemaphoreType.DMA((4,)),
        ],
        token,
        hidden,
        weight,
        out_specs=[ANY] * 4,
    )


def add_kernel(a, b, out):
    out[...] = (a[...].astype(F32) + b[...].astype(F32)).astype(BF16)


def add(token, a, b):
    out = jax.ShapeDtypeStruct(a.shape, BF16)
    return call(add_kernel, [out], [VMEM, VMEM], [], token, a, b, out_specs=[VMEM])


def add_middle_kernel(p, lo, hi, out):
    cut = lo.shape[0]
    middle = in_middle()
    for rows, b in ((pl.ds(0, cut), lo), (pl.ds(cut, hi.shape[0]), hi)):
        out[rows] = (p[rows].astype(F32) + jnp.where(middle, b[...].astype(F32), 0.0)).astype(BF16)


def add_middle(token, p, lo, hi):
    out = jax.ShapeDtypeStruct(p.shape, p.dtype)
    return call(add_middle_kernel, [out], [VMEM] * 3, [], token, p, lo, hi, out_specs=[VMEM])


def low_kernel(hidden, y0, y1, y2, y3, code, out, h_buf, w_buf, acc, h_sem, w_sem):
    rows, depth = hidden.shape
    step = depth // PIECES
    h_copies, w_copies = [], []
    for k in range(PIECES):
        span = pl.ds(k * step, step)
        h_copies += copy_in([(hidden.at[:, span], h_buf.at[:, span])], h_sem.at[pl.ds(k, 1)])
        for p, y in enumerate((y0, y1, y2, y3)):
            pair = (y.at[span], w_buf.at[span, pl.ds(p * LANES, LANES)])
            w_copies += copy_in([pair], w_sem.at[pl.ds(4 * k + p, 1)])
    for k in range(PIECES):
        h_copies[k].wait()
        for p in range(4):
            w_copies[4 * k + p].wait()
        span = pl.ds(k * step, step)
        product = jnp.dot(h_buf[:, span], w_buf[span], preferred_element_type=F32)
        if k == 0:
            acc[...] = product
        else:
            acc[...] += product
    half = rows // 2
    width = LANES // 2
    tile = min(256, half)
    owner = lax.broadcasted_iota(jnp.int32, (tile, 4 * LANES), 1) // width
    lane = lax.broadcasted_iota(jnp.int32, (tile, LANES), 1)

    def own_columns(at):
        mine = jnp.where(owner == code[at] // LANES, acc[at], 0.0)
        both = mine[:, :LANES]
        for p in range(1, 4):
            both = both + mine[:, p * LANES : (p + 1) * LANES]
        return both + pltpu.roll(both, width, 1)

    for t in range(half // tile):
        upper, lower = own_columns(pl.ds(t * tile, tile)), own_columns(pl.ds(half + t * tile, tile))
        out[pl.ds(t * tile, tile)] = jnp.where(lane < width, upper, lower).astype(BF16)


def low_product(token, hidden, ys, code):
    rows, depth = hidden.shape
    return call(
        low_kernel,
        [jax.ShapeDtypeStruct((rows // 2, LANES), BF16)],
        [ANY] * 5 + [VMEM],
        [
            pltpu.VMEM((rows, depth), BF16),
            pltpu.VMEM((depth, 4 * LANES), BF16),
            pltpu.VMEM((rows, 4 * LANES), F32),
            pltpu.SemaphoreType.DMA((PIECES,)),
            pltpu.SemaphoreType.DMA((4 * PIECES,)),
        ],
        token,
        hidden,
        *ys,
        code,
        out_specs=[VMEM],
    )


def up_kernel(hidden, weight, low, outer, y0, y1, y2, y3, code, out, h_buf, w_buf, u_buf, h_sem, w_sem, sem):
    rows, cols = out.shape
    copies = fetch(hidden, weight, 0, rows, 3, h_buf, w_buf, h_sem, w_sem)
    ups = copy_in([(y, u_buf.at[pl.ds(p * LANES, LANES)]) for p, y in enumerate((y0, y1, y2, y3))], sem)
    out[...] = product(h_buf, w_buf, 0, rows, copies)
    for c in ups:
        c.wait()
    middle = in_middle()
    width = LANES // 2
    half = rows // 2
    tile = min(256, half)
    column = lax.broadcasted_iota(jnp.int32, (tile, 4 * LANES), 1) // width
    lane = lax.broadcasted_iota(jnp.int32, (tile, LANES), 1)
    for t in range(rows // tile):
        at = pl.ds(t * tile, tile)
        hi = t * tile >= half
        packed = pl.ds(t * tile - (half if hi else 0), tile)
        mine = jnp.where(middle, low[packed].astype(F32), outer[packed].astype(F32))
        turned = pltpu.roll(mine, width, 1)
        mine = jnp.where(lane < width, turned, mine) if hi else jnp.where(lane < width, mine, turned)
        live = lax.rem(code[at], LANES)
        mine = mine * (width / (2.0 * live.astype(F32)))
        mine = jnp.where(lax.rem(lane, width) < live, mine, 0.0)
        spread = jnp.concatenate([mine] * 4, axis=1)
        spread = jnp.where(column == code[at] // LANES, spread, 0.0).astype(BF16)
        out[at] += jnp.dot(spread, u_buf[...], preferred_element_type=F32)


def own_and_up(token, hidden, weight, low, outer, ys, code):
    rows, depth = hidden.shape
    cols = weight.shape[1] // 4
    return call(
        up_kernel,
        [jax.ShapeDtypeStruct((rows, cols), F32)],
        [ANY] * 2 + [VMEM] * 2 + [ANY] * 4 + [VMEM],
        [
            pltpu.VMEM((rows, depth), BF16),
            pltpu.VMEM((depth, cols), BF16),
            pltpu.VMEM((4 * LANES, cols), BF16),
            pltpu.SemaphoreType.DMA((PIECES,)),
            pltpu.SemaphoreType.DMA((PIECES,)),
            pltpu.SemaphoreType.DMA((4,)),
        ],
        token,
        hidden,
        weight,
        low,
        outer,
        *ys,
        code,
        out_specs=[VMEM],
    )


def inner_kernel(total, lo, hi, out):
    cut = lo.shape[0]
    middle = in_middle()
    for rows, b in ((pl.ds(0, cut), lo), (pl.ds(cut, hi.shape[0]), hi)):
        out[rows] = total[rows] + jnp.where(middle, b[...].astype(F32), 0.0)


def inner_sum(token, total, lo, hi):
    out = jax.ShapeDtypeStruct(total.shape, F32)
    return call(inner_kernel, [out], [VMEM] * 3, [], token, total, lo, hi, out_specs=[VMEM])


def last_kernel(total, m, out):
    out[...] = (total[...] + m[...].astype(F32)).astype(BF16)


def last_sum(token, total, m):
    out = jax.ShapeDtypeStruct(total.shape, BF16)
    return call(last_kernel, [out], [VMEM] * 2, [], token, total, m, out_specs=[VMEM])[0]


def by_adapter(row_adapter, values):
    every = jnp.arange(values.shape[0], dtype=jnp.int32)
    return jnp.sum(jnp.where(row_adapter == every[None, :], values[None, :], 0), axis=1, keepdims=True)


def line_of_four(hidden, weight, down, up, row_adapter, rank_of_adapter, adapter_storage_slot):
    rows = hidden.shape[0]
    start = rows // 2
    at = lax.axis_index("dp")
    per_index = adapter_storage_slot.shape[0] // 4

    def cross(v):
        return lax.ppermute(v, "tensor", [(0, 1), (1, 0), (2, 3), (3, 2)])

    def inner(v):
        return lax.ppermute(v, "tensor", [(1, 2), (2, 1)])

    def swap(v, bit):
        return lax.ppermute(v, "dp", [(i, i ^ bit) for i in range(4)])

    places = ((adapter_storage_slot // per_index) ^ at) * per_index + adapter_storage_slot % per_index
    code = by_adapter(row_adapter, places * LANES + rank_of_adapter)

    down2, down1 = swap(down, 2), swap(down, 1)
    up2, up1 = swap(up, 2), swap(up, 1)

    p0a, t = first_product(hidden, weight, start)
    a1a = cross(p0a)
    p0b, p1a, p1b, p2, t = next_products(t, hidden, weight, start)
    a1b = cross(p0b)
    a2a = cross(p1a)
    v, t = add(t, p0a, a1a)
    b1a = inner(v)
    down2, up2, t = relay(t, down2, up2)
    downs = (down, down1, down2, swap(down2, 1))
    ups = (up, up1, up2, swap(up2, 1))
    low, t = low_product(t, hidden, downs, code)
    e1 = cross(low)
    p1b, t = relay(t, p1b)
    a2b = cross(p1b)
    v, t = add(t, p0b, a1b)
    b1b = inner(v)
    low, t = add(t, low, e1)
    e2 = inner(low)
    v, t = add(t, p1a, a2a)
    b2a = inner(v)
    v, t = add_middle(t, p2, b1a, b1b)
    m3 = cross(v)
    low, t = add(t, low, e2)
    e3 = cross(low)
    v, t = add(t, p1b, a2b)
    b2b = inner(v)
    total, t = own_and_up(t, hidden, weight, low, e3, ups, code)
    total, t = inner_sum(t, total, b2a, b2b)
    return last_sum(t, total, m3)


def any_line(hidden, weight, down, up, row_adapter, rank_of_adapter, adapter_storage_slot):
    rows = hidden.shape[0]
    adapters = rank_of_adapter.shape[0]
    width = down.shape[1] * lax.axis_size("dp") // adapters
    slot = by_adapter(row_adapter, adapter_storage_slot)
    rank = by_adapter(row_adapter, rank_of_adapter)
    chosen = slot == jnp.arange(adapters, dtype=jnp.int32)[None, :]
    partial = jnp.dot(hidden, weight, preferred_element_type=F32).astype(BF16)
    base = lax.psum_scatter(partial, "tensor", scatter_dimension=1, tiled=True).astype(F32)
    downs = lax.all_gather(down, "dp", axis=1, tiled=True)
    product = jnp.dot(hidden, downs, preferred_element_type=F32)
    low = jnp.einsum("rac,ra->rc", product.reshape(rows, adapters, width), chosen.astype(F32))
    low = lax.psum(low.astype(BF16), "tensor").astype(F32)
    live = jnp.arange(width, dtype=jnp.int32)[None, :] < rank
    scaling = width / (2.0 * rank.astype(F32))
    low_rank = jnp.where(live, low * scaling, F32(0.0)).astype(BF16)
    spread = jnp.where(chosen[:, :, None], low_rank[:, None, :], jnp.zeros((), BF16)).reshape(rows, -1)
    ups = lax.all_gather(up, "dp", axis=0, tiled=True)
    return (base + jnp.dot(spread, ups, preferred_element_type=F32)).astype(BF16)


def on_device(hidden, weight, down, up, *rest):
    fits = (
        lax.axis_size("tensor") == 4
        and lax.axis_size("dp") == 4
        and down.shape[1] == LANES
        and up.shape[0] == LANES
        and rest[1].shape[0] == 8
        and hidden.shape[0] % 512 == 0
        and hidden.shape[1] % (PIECES * LANES) == 0
        and up.shape[1] == 4 * LANES
    )
    return (line_of_four if fits else any_line)(hidden, weight, down, up, *rest)


def solution(mesh):
    return jax.shard_map(
        on_device,
        mesh=mesh,
        in_specs=(
            P(("groups", "dp"), "tensor"),
            P("tensor", None),
            P("tensor", "dp"),
            P("dp", "tensor"),
            P(("groups", "dp"), None),
            P(),
            P(),
        ),
        out_specs=P(("groups", "dp"), "tensor"),
        check_vma=False,
    )
```

```python
import functools

import jax
import jax.numpy as jnp
from jax import lax
from jax.experimental import pallas as pl
from jax.experimental.pallas import tpu as pltpu
from jax.sharding import PartitionSpec as P

F32 = jnp.float32
BF16 = jnp.bfloat16
LANES = 128
PIECES = 4
ANY = pl.BlockSpec(memory_space=pl.ANY)
VMEM = pl.BlockSpec(memory_space=pltpu.VMEM)
PARAMS = pltpu.CompilerParams(vmem_limit_bytes=64 * 1024 * 1024 - 128 * 1024)
COST = pl.CostEstimate(flops=1, bytes_accessed=1, transcendentals=0)


def call(kernel, outs, in_specs, scratch, token, *args, out_specs, aliases=None):
    n_in, n_out = len(args), len(outs)
    aliases = dict(aliases or {})
    if token is not None:
        args += (token,)
        in_specs = [*in_specs, ANY]
        aliases[n_in] = n_out

    def body(*refs):
        given = refs[:n_in]
        rest = refs[len(args) :]
        kernel(*given, *rest[:n_out], *rest[n_out + 1 :])

    return pl.pallas_call(
        body,
        out_shape=(*outs, jax.ShapeDtypeStruct((8, LANES), F32)),
        in_specs=in_specs,
        out_specs=(*out_specs, ANY),
        scratch_shapes=scratch,
        input_output_aliases=aliases,
        compiler_params=PARAMS,
        cost_estimate=COST,
    )(*args)


def relay(token, *arrays):
    return call(
        lambda *refs: None,
        [jax.ShapeDtypeStruct(a.shape, a.dtype) for a in arrays],
        [ANY] * len(arrays),
        [],
        token,
        *arrays,
        out_specs=[ANY] * len(arrays),
        aliases={i: i for i in range(len(arrays))},
    )


def in_middle():
    me = lax.axis_index("tensor")
    return jnp.logical_and(me > 0, me < 3)


def block_of(phase):
    me = lax.axis_index("tensor")
    if phase == 0:
        return jnp.where(me < 2, 3, 0)
    if phase == 1:
        return jnp.where(me < 2, 2, 1)
    if phase == 2:
        return me + 1 - 2 * lax.rem(me, 2)
    return me


def copy_in(pairs, sems):
    copies = [pltpu.make_async_copy(a, b, sems.at[i]) for i, (a, b) in enumerate(pairs)]
    for c in copies:
        c.start()
    return copies


def fetch(hidden, weight, lo, rows, phase, first_row, h_buf, w_buf, h_sem, w_sem):
    depth, cols = w_buf.shape
    step = depth // PIECES
    first = pl.multiple_of(block_of(phase) * cols, cols)
    h_copies, w_copies = [], []
    for k in range(PIECES):
        span = pl.ds(k * step, step)
        if h_sem is not None:
            pair = (hidden.at[pl.ds(lo, rows), span], h_buf.at[pl.ds(lo - first_row, rows), span])
            h_copies += copy_in([pair], h_sem.at[pl.ds(k, 1)])
        pair = (weight.at[span, pl.ds(first, cols)], w_buf.at[span])
        w_copies += copy_in([pair], w_sem.at[pl.ds(k, 1)])
    return h_copies, w_copies


def product(h_buf, w_buf, lo, rows, copies):
    h_copies, w_copies = copies
    step = w_buf.shape[0] // PIECES
    total = None
    for k in range(PIECES):
        if h_copies:
            h_copies[k].wait()
        if w_copies:
            w_copies[k].wait()
        span = pl.ds(k * step, step)
        term = jnp.dot(h_buf[pl.ds(lo, rows), span], w_buf[span], preferred_element_type=F32)
        total = term if total is None else total + term
    return total


def products_kernel(jobs, count, hidden, weight, *rest):
    outs, (h_buf, w_buf, buf, h_sem, w_sem, o_sem) = rest[:count], rest[count:]
    first = min(job[1] for job in jobs)
    copies, loaded = [], set()
    for j, (phase, lo, rows, _, _) in enumerate(jobs):
        fresh = not set(range(lo, lo + rows)) <= loaded
        loaded |= set(range(lo, lo + rows))
        sems = h_sem.at[j] if fresh else None
        copies.append(fetch(hidden, weight, lo, rows, phase, first, h_buf, w_buf.at[j], sems, w_sem.at[j]))
    sent = []
    for j, (_, lo, rows, o, at) in enumerate(jobs):
        value = product(h_buf, w_buf.at[j], lo - first, rows, copies[j])
        buf[j, pl.ds(0, rows)] = value.astype(BF16)
        pair = (buf.at[j, pl.ds(0, rows)], outs[o].at[pl.ds(at, rows)])
        sent += copy_in([pair], o_sem.at[pl.ds(j, 1)])
    for c in sent:
        c.wait()


def products(token, hidden, weight, jobs, heights):
    depth = hidden.shape[1]
    cols = weight.shape[1] // 4
    first = min(job[1] for job in jobs)
    last = max(job[1] + job[2] for job in jobs)
    most = max(job[2] for job in jobs)
    count = len(jobs)
    return call(
        functools.partial(products_kernel, jobs, len(heights)),
        [jax.ShapeDtypeStruct((rows, cols), BF16) for rows in heights],
        [ANY] * 2,
        [
            pltpu.VMEM((last - first, depth), BF16),
            pltpu.VMEM((count, depth, cols), BF16),
            pltpu.VMEM((count, most, cols), BF16),
            pltpu.SemaphoreType.DMA((count, PIECES)),
            pltpu.SemaphoreType.DMA((count, PIECES)),
            pltpu.SemaphoreType.DMA((count,)),
        ],
        token,
        hidden,
        weight,
        out_specs=[ANY] * len(heights),
    )


def add_kernel(a, b, *outs):
    at = 0
    for out in outs:
        rows = pl.ds(at, out.shape[0])
        out[...] = (a[rows].astype(F32) + b[rows].astype(F32)).astype(BF16)
        at += out.shape[0]


def add(token, a, b, heights=None):
    outs = [jax.ShapeDtypeStruct((rows, a.shape[1]), BF16) for rows in heights or (a.shape[0],)]
    return call(add_kernel, outs, [VMEM, VMEM], [], token, a, b, out_specs=[VMEM] * len(outs))


def add_middle_kernel(lo, spans, p, *rest):
    count = len(spans)
    givens, (out, p_buf, g_buf, sem) = rest[:count], rest[count:]
    pairs, to = [(p.at[pl.ds(lo, out.shape[0])], p_buf)], 0
    for g, (at, rows) in zip(givens, spans):
        pairs.append((g.at[pl.ds(at, rows)], g_buf.at[pl.ds(to, rows)]))
        to += rows
    for c in copy_in(pairs, sem):
        c.wait()
    other = jnp.where(in_middle(), g_buf[...].astype(F32), 0.0)
    out[...] = (p_buf[...].astype(F32) + other).astype(BF16)


def add_middle(token, p, lo, givens, spans):
    shape = (sum(rows for _, rows in spans), p.shape[1])
    return call(
        functools.partial(add_middle_kernel, lo, spans),
        [jax.ShapeDtypeStruct(shape, BF16)],
        [ANY] * (1 + len(givens)),
        [pltpu.VMEM(shape, BF16)] * 2 + [pltpu.SemaphoreType.DMA((1 + len(givens),))],
        token,
        p,
        *givens,
        out_specs=[VMEM],
    )


def low_kernel(hidden, y0, y1, y2, y3, code, _, out, h_buf, w_buf, acc, low, h_sem, w_sem, o_sem):
    rows, depth = hidden.shape
    step = depth // PIECES
    h_copies, w_copies = [], []
    for k in range(PIECES):
        span = pl.ds(k * step, step)
        h_copies += copy_in([(hidden.at[:, span], h_buf.at[:, span])], h_sem.at[pl.ds(k, 1)])
        for p, y in enumerate((y0, y1, y2, y3)):
            pair = (y.at[span], w_buf.at[span, pl.ds(p * LANES, LANES)])
            w_copies += copy_in([pair], w_sem.at[pl.ds(4 * k + p, 1)])
    for k in range(PIECES):
        h_copies[k].wait()
        for p in range(4):
            w_copies[4 * k + p].wait()
        span = pl.ds(k * step, step)
        product = jnp.dot(h_buf[:, span], w_buf[span], preferred_element_type=F32)
        if k == 0:
            acc[...] = product
        else:
            acc[...] += product
    width = LANES // 2
    tile = rows // 8
    owner = lax.broadcasted_iota(jnp.int32, (tile, 4 * LANES), 1) // width
    lane = lax.broadcasted_iota(jnp.int32, (tile, LANES), 1)

    def own_columns(at):
        mine = jnp.where(owner == code[at] // LANES, acc[at], 0.0)
        both = mine[:, :LANES]
        for p in range(1, 4):
            both = both + mine[:, p * LANES : (p + 1) * LANES]
        return both + pltpu.roll(both, width, 1)

    for t in range(4):
        first, second = own_columns(pl.ds(2 * t * tile, tile)), own_columns(pl.ds((2 * t + 1) * tile, tile))
        low[:, pl.ds(t * LANES, LANES)] = jnp.where(lane < width, first, second).astype(BF16)
    for c in copy_in([(low, out.at[pl.ds(out.shape[0] - tile, tile)])], o_sem):
        c.wait()


def low_product(token, hidden, ys, code, under):
    rows, depth = hidden.shape
    return call(
        low_kernel,
        [jax.ShapeDtypeStruct(under.shape, BF16)],
        [ANY] * 5 + [VMEM, ANY],
        [
            pltpu.VMEM((rows, depth), BF16),
            pltpu.VMEM((depth, 4 * LANES), BF16),
            pltpu.VMEM((rows, 4 * LANES), F32),
            pltpu.VMEM((rows // 8, 4 * LANES), BF16),
            pltpu.SemaphoreType.DMA((PIECES,)),
            pltpu.SemaphoreType.DMA((4 * PIECES,)),
            pltpu.SemaphoreType.DMA((1,)),
        ],
        token,
        hidden,
        *ys,
        code,
        under,
        out_specs=[ANY],
        aliases={6: 0},
    )


def own_kernel(hidden, weight, out, h_buf, w_buf, h_sem, w_sem):
    rows = hidden.shape[0]
    copies = fetch(hidden, weight, 0, rows, 3, 0, h_buf, w_buf, h_sem, w_sem)
    out[...] = product(h_buf, w_buf, 0, rows, copies)


def own_product(token, hidden, weight):
    rows, depth = hidden.shape
    cols = weight.shape[1] // 4
    return call(
        own_kernel,
        [jax.ShapeDtypeStruct((rows, cols), F32)],
        [ANY] * 2,
        [
            pltpu.VMEM((rows, depth), BF16),
            pltpu.VMEM((depth, cols), BF16),
            pltpu.SemaphoreType.DMA((PIECES,)),
            pltpu.SemaphoreType.DMA((PIECES,)),
        ],
        token,
        hidden,
        weight,
        out_specs=[VMEM],
    )


def up_kernel(own, low, other, y0, y1, y2, y3, code, b, m, out, rest, u_buf, sem):
    rows, cols = own.shape
    ups = copy_in([(y, u_buf.at[pl.ds(p * LANES, LANES)]) for p, y in enumerate((y0, y1, y2, y3))], sem)
    for c in ups:
        c.wait()
    middle = in_middle()
    width = LANES // 2
    half = rows // 2
    tile = rows // 8
    column = lax.broadcasted_iota(jnp.int32, (tile, 4 * LANES), 1) // width
    lane = lax.broadcasted_iota(jnp.int32, (tile, LANES), 1)
    b_at = b.shape[0] - half
    for t in range(4):
        lanes = pl.ds(t * LANES, LANES)
        pair = low[:, lanes].astype(F32) + other[:, lanes].astype(F32)
        turned = pltpu.roll(pair, width, 1)
        spreads = []
        for k in range(2):
            rows_at = pl.ds((2 * t + k) * tile, tile)
            mine = jnp.where(lane < width, turned, pair) if k else jnp.where(lane < width, pair, turned)
            live = lax.rem(code[rows_at], LANES)
            mine = mine * (width / (2.0 * live.astype(F32)))
            mine = jnp.where(lax.rem(lane, width) < live, mine, 0.0)
            spread = jnp.concatenate([mine] * 4, axis=1)
            spreads.append(jnp.where(column == code[rows_at] // LANES, spread, 0.0).astype(BF16))
        at = pl.ds(2 * t * tile, 2 * tile)
        spread = jnp.concatenate(spreads, axis=0)
        total = own[at] + jnp.dot(spread, u_buf[...], preferred_element_type=F32)
        if t < 2:
            inner = b[pl.ds(b_at + 2 * t * tile, 2 * tile)].astype(F32)
            total = total + jnp.where(middle, inner, 0.0)
            out[at] = (total + m[at].astype(F32)).astype(BF16)
        else:
            rest[pl.ds((2 * t - 4) * tile, 2 * tile)] = total


def up_sum(token, own, low, other, ys, code, b, m):
    rows, cols = own.shape
    return call(
        up_kernel,
        [jax.ShapeDtypeStruct((rows, cols), BF16), jax.ShapeDtypeStruct((rows // 2, cols), F32)],
        [VMEM] * 3 + [ANY] * 4 + [VMEM] * 3,
        [
            pltpu.VMEM((4 * LANES, cols), BF16),
            pltpu.SemaphoreType.DMA((4,)),
        ],
        token,
        own,
        low,
        other,
        *ys,
        code,
        b,
        m,
        out_specs=[VMEM] * 2,
    )


def last_kernel(done, rest, b, m, out, buf, sem):
    half = rest.shape[0]
    total = rest[...] + jnp.where(in_middle(), b[...].astype(F32), 0.0)
    buf[...] = (total + m[...].astype(F32)).astype(BF16)
    for c in copy_in([(buf, out.at[pl.ds(half, half)])], sem):
        c.wait()


def last_sum(token, done, rest, b, m):
    return call(
        last_kernel,
        [jax.ShapeDtypeStruct(done.shape, BF16)],
        [ANY] + [VMEM] * 3,
        [pltpu.VMEM(rest.shape, BF16), pltpu.SemaphoreType.DMA((1,))],
        token,
        done,
        rest,
        b,
        m,
        out_specs=[ANY],
        aliases={0: 0},
    )[0]


def by_adapter(row_adapter, values):
    every = jnp.arange(values.shape[0], dtype=jnp.int32)
    return jnp.sum(jnp.where(row_adapter == every[None, :], values[None, :], 0), axis=1, keepdims=True)


def line_of_four(hidden, weight, down, up, row_adapter, rank_of_adapter, adapter_storage_slot):
    rows = hidden.shape[0]
    half = rows // 2
    at = lax.axis_index("dp")
    per_index = adapter_storage_slot.shape[0] // 4

    def send(v, pairs):
        return lax.ppermute(v, "tensor", pairs)

    near = [(0, 1), (1, 0), (2, 3), (3, 2)]
    middle = [(1, 2), (2, 1)]
    two = [(0, 2), (2, 0), (1, 3), (3, 1)]

    def swap(v, bit):
        return lax.ppermute(v, "dp", [(i, i ^ bit) for i in range(4)])

    places = ((adapter_storage_slot // per_index) ^ at) * per_index + adapter_storage_slot % per_index
    code = by_adapter(row_adapter, places * LANES + rank_of_adapter)

    down2, down1 = swap(down, 2), swap(down, 1)
    up2, up1 = swap(up, 2), swap(up, 1)

    cut = rows * 3 // 4
    after = rows - cut
    p0a, t = products(None, hidden, weight, [(0, 0, cut, 0, 0)], [cut])
    a1a = send(p0a, near)
    jobs = [(1, 0, half, 0, after), (1, half, half, 1, 0), (0, cut, after, 0, 0), (2, 0, rows, 2, 0)]
    p01, p1l, p2, t = products(t, hidden, weight, jobs, [after + half, half + rows // 8, rows])
    a12 = send(p01, near)
    down2, t = relay(t, down2)
    downs = (down, down1, down2, swap(down2, 1))
    v, t = add(t, p0a, a1a)
    b1a = send(v, middle)
    p1l, t = low_product(t, hidden, downs, code, p1l)
    a2l = send(p1l, near)
    v, t = add(t, p01, a12)
    b12 = send(v, middle)
    v, t = add_middle(t, p2, 0, (b1a,), [(0, half)])
    m3a = send(v, near)
    own, t = own_product(t, hidden, weight)
    up2, t = relay(t, up2)
    ups = (up, up1, up2, swap(up2, 1))
    v, low, t = add(t, p1l, a2l, [half, rows // 8])
    b2b = send(v, middle)
    e2 = send(low, two)
    m, t = add_middle(t, p2, half, (b1a, b12), [(half, cut - half), (0, after)])
    m, m3a, e2, t = relay(t, m, m3a, e2)
    m3b = send(m, near)
    out, rest, t = up_sum(t, own, low, e2, ups, code, b12, m3a)
    return last_sum(t, out, rest, b2b, m3b)


def any_line(hidden, weight, down, up, row_adapter, rank_of_adapter, adapter_storage_slot):
    rows = hidden.shape[0]
    adapters = rank_of_adapter.shape[0]
    width = down.shape[1] * lax.axis_size("dp") // adapters
    slot = by_adapter(row_adapter, adapter_storage_slot)
    rank = by_adapter(row_adapter, rank_of_adapter)
    chosen = slot == jnp.arange(adapters, dtype=jnp.int32)[None, :]
    partial = jnp.dot(hidden, weight, preferred_element_type=F32).astype(BF16)
    base = lax.psum_scatter(partial, "tensor", scatter_dimension=1, tiled=True).astype(F32)
    downs = lax.all_gather(down, "dp", axis=1, tiled=True)
    product = jnp.dot(hidden, downs, preferred_element_type=F32)
    low = jnp.einsum("rac,ra->rc", product.reshape(rows, adapters, width), chosen.astype(F32))
    low = lax.psum(low.astype(BF16), "tensor").astype(F32)
    live = jnp.arange(width, dtype=jnp.int32)[None, :] < rank
    scaling = width / (2.0 * rank.astype(F32))
    low_rank = jnp.where(live, low * scaling, F32(0.0)).astype(BF16)
    spread = jnp.where(chosen[:, :, None], low_rank[:, None, :], jnp.zeros((), BF16)).reshape(rows, -1)
    ups = lax.all_gather(up, "dp", axis=0, tiled=True)
    return (base + jnp.dot(spread, ups, preferred_element_type=F32)).astype(BF16)


def on_device(hidden, weight, down, up, *rest):
    fits = (
        lax.axis_size("tensor") == 4
        and lax.axis_size("dp") == 4
        and down.shape[1] == LANES
        and up.shape[0] == LANES
        and rest[1].shape[0] == 8
        and hidden.shape[0] % 1024 == 0
        and hidden.shape[1] % (PIECES * LANES) == 0
        and up.shape[1] == 4 * LANES
    )
    return (line_of_four if fits else any_line)(hidden, weight, down, up, *rest)


def solution(mesh):
    return jax.shard_map(
        on_device,
        mesh=mesh,
        in_specs=(
            P(("groups", "dp"), "tensor"),
            P("tensor", None),
            P("tensor", "dp"),
            P("dp", "tensor"),
            P(("groups", "dp"), None),
            P(),
            P(),
        ),
        out_specs=P(("groups", "dp"), "tensor"),
        check_vma=False,
    )
```

```python
import functools

import jax
import jax.numpy as jnp
from jax import lax
from jax.experimental import pallas as pl
from jax.experimental.pallas import tpu as pltpu
from jax.sharding import PartitionSpec as P

F32 = jnp.float32
BF16 = jnp.bfloat16
LANES = 128
PIECES = 4
LOW_PIECES = 2
ANY = pl.BlockSpec(memory_space=pl.ANY)
VMEM = pl.BlockSpec(memory_space=pltpu.VMEM)
PARAMS = pltpu.CompilerParams(vmem_limit_bytes=64 * 1024 * 1024 - 128 * 1024)
COST = pl.CostEstimate(flops=1, bytes_accessed=1, transcendentals=0)
MORE = pl.CostEstimate(flops=1 << 32, bytes_accessed=1 << 20, transcendentals=0)


def call(kernel, outs, in_specs, scratch, token, *args, out_specs, aliases=None, cost=COST):
    n_in, n_out = len(args), len(outs)
    aliases = dict(aliases or {})
    if token is not None:
        args += (token,)
        in_specs = [*in_specs, ANY]
        aliases[n_in] = n_out

    def body(*refs):
        given = refs[:n_in]
        rest = refs[len(args) :]
        kernel(*given, *rest[:n_out], *rest[n_out + 1 :])

    return pl.pallas_call(
        body,
        out_shape=(*outs, jax.ShapeDtypeStruct((8, LANES), F32)),
        in_specs=in_specs,
        out_specs=(*out_specs, ANY),
        scratch_shapes=scratch,
        input_output_aliases=aliases,
        compiler_params=PARAMS,
        cost_estimate=cost,
    )(*args)


def relay(token, *arrays):
    return call(
        lambda *refs: None,
        [jax.ShapeDtypeStruct(a.shape, a.dtype) for a in arrays],
        [ANY] * len(arrays),
        [],
        token,
        *arrays,
        out_specs=[ANY] * len(arrays),
        aliases={i: i for i in range(len(arrays))},
    )


def in_middle():
    me = lax.axis_index("tensor")
    return jnp.logical_and(me > 0, me < 3)


def block_of(phase):
    me = lax.axis_index("tensor")
    if phase == 0:
        return jnp.where(me < 2, 3, 0)
    if phase == 1:
        return jnp.where(me < 2, 2, 1)
    if phase == 2:
        return me + 1 - 2 * lax.rem(me, 2)
    return me


def copy_in(pairs, sems):
    copies = [pltpu.make_async_copy(a, b, sems.at[i]) for i, (a, b) in enumerate(pairs)]
    for c in copies:
        c.start()
    return copies


def fetch(hidden, weight, lo, rows, phase, first_row, h_buf, w_buf, h_sem, w_sem):
    depth, cols = w_buf.shape
    pieces = w_sem.shape[0]
    step = depth // pieces
    first = pl.multiple_of(block_of(phase) * cols, cols)
    h_copies, w_copies = [], []
    for k in range(pieces):
        span = pl.ds(k * step, step)
        if h_sem is not None:
            pair = (hidden.at[pl.ds(lo, rows), span], h_buf.at[pl.ds(lo - first_row, rows), span])
            h_copies += copy_in([pair], h_sem.at[pl.ds(k, 1)])
        pair = (weight.at[span, pl.ds(first, cols)], w_buf.at[span])
        w_copies += copy_in([pair], w_sem.at[pl.ds(k, 1)])
    return h_copies, w_copies


def product(h_buf, w_buf, lo, rows, copies):
    h_copies, w_copies = copies
    pieces = len(copies[1])
    step = w_buf.shape[0] // pieces
    total = None
    for k in range(pieces):
        if h_copies:
            h_copies[k].wait()
        if w_copies:
            w_copies[k].wait()
        span = pl.ds(k * step, step)
        term = jnp.dot(h_buf[pl.ds(lo, rows), span], w_buf[span], preferred_element_type=F32)
        total = term if total is None else total + term
    return total


def products_kernel(jobs, count, hidden, weight, *rest):
    outs, (h_buf, w_buf, buf, h_sem, w_sem, o_sem) = rest[:count], rest[count:]
    first = min(job[1] for job in jobs)
    copies, loaded = [], set()
    for j, (phase, lo, rows, _, _) in enumerate(jobs):
        fresh = not set(range(lo, lo + rows)) <= loaded
        loaded |= set(range(lo, lo + rows))
        sems = h_sem.at[j] if fresh else None
        copies.append(fetch(hidden, weight, lo, rows, phase, first, h_buf, w_buf.at[j], sems, w_sem.at[j]))
    sent = []
    for j, (_, lo, rows, o, at) in enumerate(jobs):
        value = product(h_buf, w_buf.at[j], lo - first, rows, copies[j])
        buf[j, pl.ds(0, rows)] = value.astype(BF16)
        pair = (buf.at[j, pl.ds(0, rows)], outs[o].at[pl.ds(at, rows)])
        sent += copy_in([pair], o_sem.at[pl.ds(j, 1)])
    for c in sent:
        c.wait()


def products(token, hidden, weight, jobs, heights):
    depth = hidden.shape[1]
    cols = weight.shape[1] // 4
    first = min(job[1] for job in jobs)
    last = max(job[1] + job[2] for job in jobs)
    most = max(job[2] for job in jobs)
    count = len(jobs)
    pieces = PIECES * 2 if count == 1 else PIECES
    return call(
        functools.partial(products_kernel, jobs, len(heights)),
        [jax.ShapeDtypeStruct((rows, cols), BF16) for rows in heights],
        [ANY] * 2,
        [
            pltpu.VMEM((last - first, depth), BF16),
            pltpu.VMEM((count, depth, cols), BF16),
            pltpu.VMEM((count, most, cols), BF16),
            pltpu.SemaphoreType.DMA((count, pieces)),
            pltpu.SemaphoreType.DMA((count, pieces)),
            pltpu.SemaphoreType.DMA((count,)),
        ],
        token,
        hidden,
        weight,
        out_specs=[ANY] * len(heights),
    )


def add_kernel(a, b, *outs):
    at = 0
    for out in outs:
        rows = pl.ds(at, out.shape[0])
        out[...] = (a[rows].astype(F32) + b[rows].astype(F32)).astype(BF16)
        at += out.shape[0]


def add(token, a, b, heights=None, cost=COST):
    outs = [jax.ShapeDtypeStruct((rows, a.shape[1]), BF16) for rows in heights or (a.shape[0],)]
    return call(
        add_kernel, outs, [VMEM, VMEM], [], token, a, b, out_specs=[VMEM] * len(outs), cost=cost
    )


def add_middle_kernel(lo, spans, p, *rest):
    count = len(spans)
    givens, (out, p_buf, g_buf, sem) = rest[:count], rest[count:]
    pairs, to = [(p.at[pl.ds(lo, out.shape[0])], p_buf)], 0
    for g, (at, rows) in zip(givens, spans):
        pairs.append((g.at[pl.ds(at, rows)], g_buf.at[pl.ds(to, rows)]))
        to += rows
    for c in copy_in(pairs, sem):
        c.wait()
    other = jnp.where(in_middle(), g_buf[...].astype(F32), 0.0)
    out[...] = (p_buf[...].astype(F32) + other).astype(BF16)


def add_middle(token, p, lo, givens, spans):
    shape = (sum(rows for _, rows in spans), p.shape[1])
    return call(
        functools.partial(add_middle_kernel, lo, spans),
        [jax.ShapeDtypeStruct(shape, BF16)],
        [ANY] * (1 + len(givens)),
        [pltpu.VMEM(shape, BF16)] * 2 + [pltpu.SemaphoreType.DMA((1 + len(givens),))],
        token,
        p,
        *givens,
        out_specs=[VMEM],
    )


def low_kernel(hidden, y0, y1, y2, y3, code, _, out, h_buf, w_buf, acc, low, h_sem, w_sem, o_sem):
    rows, depth = hidden.shape
    step = depth // LOW_PIECES
    h_copies, w_copies = [], []
    for k in range(LOW_PIECES):
        span = pl.ds(k * step, step)
        h_copies += copy_in([(hidden.at[:, span], h_buf.at[:, span])], h_sem.at[pl.ds(k, 1)])
        for p, y in enumerate((y0, y1, y2, y3)):
            pair = (y.at[span], w_buf.at[span, pl.ds(p * LANES, LANES)])
            w_copies += copy_in([pair], w_sem.at[pl.ds(4 * k + p, 1)])
    for k in range(LOW_PIECES):
        h_copies[k].wait()
        for p in range(4):
            w_copies[4 * k + p].wait()
        span = pl.ds(k * step, step)
        product = jnp.dot(h_buf[:, span], w_buf[span], preferred_element_type=F32)
        if k == 0:
            acc[...] = product
        else:
            acc[...] += product
    width = LANES // 2
    tile = rows // 8
    owner = lax.broadcasted_iota(jnp.int32, (tile, 4 * LANES), 1) // width
    lane = lax.broadcasted_iota(jnp.int32, (tile, LANES), 1)

    def own_columns(at):
        mine = jnp.where(owner == code[at] // LANES, acc[at], 0.0)
        both = mine[:, :LANES]
        for p in range(1, 4):
            both = both + mine[:, p * LANES : (p + 1) * LANES]
        return both + pltpu.roll(both, width, 1)

    for t in range(4):
        first, second = own_columns(pl.ds(2 * t * tile, tile)), own_columns(pl.ds((2 * t + 1) * tile, tile))
        low[:, pl.ds(t * LANES, LANES)] = jnp.where(lane < width, first, second).astype(BF16)
    for c in copy_in([(low, out.at[pl.ds(out.shape[0] - tile, tile)])], o_sem):
        c.wait()


def low_product(token, hidden, ys, code, under):
    rows, depth = hidden.shape
    return call(
        low_kernel,
        [jax.ShapeDtypeStruct(under.shape, BF16)],
        [ANY] * 5 + [VMEM, ANY],
        [
            pltpu.VMEM((rows, depth), BF16),
            pltpu.VMEM((depth, 4 * LANES), BF16),
            pltpu.VMEM((rows, 4 * LANES), F32),
            pltpu.VMEM((rows // 8, 4 * LANES), BF16),
            pltpu.SemaphoreType.DMA((LOW_PIECES,)),
            pltpu.SemaphoreType.DMA((4 * LOW_PIECES,)),
            pltpu.SemaphoreType.DMA((1,)),
        ],
        token,
        hidden,
        *ys,
        code,
        under,
        out_specs=[ANY],
        aliases={6: 0},
    )


def own_kernel(hidden, weight, out, h_buf, w_buf, h_sem, w_sem):
    rows = hidden.shape[0]
    copies = fetch(hidden, weight, 0, rows, 3, 0, h_buf, w_buf, h_sem, w_sem)
    out[...] = product(h_buf, w_buf, 0, rows, copies)


def own_product(token, hidden, weight):
    rows, depth = hidden.shape
    cols = weight.shape[1] // 4
    return call(
        own_kernel,
        [jax.ShapeDtypeStruct((rows, cols), F32)],
        [ANY] * 2,
        [
            pltpu.VMEM((rows, depth), BF16),
            pltpu.VMEM((depth, cols), BF16),
            pltpu.SemaphoreType.DMA((PIECES,)),
            pltpu.SemaphoreType.DMA((PIECES,)),
        ],
        token,
        hidden,
        weight,
        out_specs=[VMEM],
    )


def up_kernel(own, low, other, y0, y1, y2, y3, code, b, m, out, rest, u_buf, sem):
    rows, cols = own.shape
    ups = copy_in([(y, u_buf.at[pl.ds(p * LANES, LANES)]) for p, y in enumerate((y0, y1, y2, y3))], sem)
    for c in ups:
        c.wait()
    middle = in_middle()
    width = LANES // 2
    half = rows // 2
    tile = rows // 8
    column = lax.broadcasted_iota(jnp.int32, (tile, 4 * LANES), 1) // width
    lane = lax.broadcasted_iota(jnp.int32, (tile, LANES), 1)
    b_at = b.shape[0] - half
    for t in range(4):
        lanes = pl.ds(t * LANES, LANES)
        pair = low[:, lanes].astype(F32) + other[:, lanes].astype(F32)
        turned = pltpu.roll(pair, width, 1)
        spreads = []
        for k in range(2):
            rows_at = pl.ds((2 * t + k) * tile, tile)
            mine = jnp.where(lane < width, turned, pair) if k else jnp.where(lane < width, pair, turned)
            live = lax.rem(code[rows_at], LANES)
            mine = mine * (width / (2.0 * live.astype(F32)))
            mine = jnp.where(lax.rem(lane, width) < live, mine, 0.0)
            spread = jnp.concatenate([mine] * 4, axis=1)
            spreads.append(jnp.where(column == code[rows_at] // LANES, spread, 0.0).astype(BF16))
        at = pl.ds(2 * t * tile, 2 * tile)
        spread = jnp.concatenate(spreads, axis=0)
        total = own[at] + jnp.dot(spread, u_buf[...], preferred_element_type=F32)
        if t < 2:
            inner = b[pl.ds(b_at + 2 * t * tile, 2 * tile)].astype(F32)
            total = total + jnp.where(middle, inner, 0.0)
            out[at] = (total + m[at].astype(F32)).astype(BF16)
        else:
            rest[pl.ds((2 * t - 4) * tile, 2 * tile)] = total


def up_sum(token, own, low, other, ys, code, b, m):
    rows, cols = own.shape
    return call(
        up_kernel,
        [jax.ShapeDtypeStruct((rows, cols), BF16), jax.ShapeDtypeStruct((rows // 2, cols), F32)],
        [VMEM] * 3 + [ANY] * 4 + [VMEM] * 3,
        [
            pltpu.VMEM((4 * LANES, cols), BF16),
            pltpu.SemaphoreType.DMA((4,)),
        ],
        token,
        own,
        low,
        other,
        *ys,
        code,
        b,
        m,
        out_specs=[VMEM] * 2,
        cost=MORE,
    )


def last_kernel(done, rest, b, m, out, buf, sem):
    half = rest.shape[0]
    total = rest[...] + jnp.where(in_middle(), b[...].astype(F32), 0.0)
    buf[...] = (total + m[...].astype(F32)).astype(BF16)
    for c in copy_in([(buf, out.at[pl.ds(half, half)])], sem):
        c.wait()


def last_sum(token, done, rest, b, m):
    return call(
        last_kernel,
        [jax.ShapeDtypeStruct(done.shape, BF16)],
        [ANY] + [VMEM] * 3,
        [pltpu.VMEM(rest.shape, BF16), pltpu.SemaphoreType.DMA((1,))],
        token,
        done,
        rest,
        b,
        m,
        out_specs=[ANY],
        aliases={0: 0},
    )[0]


def by_adapter(row_adapter, values):
    every = jnp.arange(values.shape[0], dtype=jnp.int32)
    return jnp.sum(jnp.where(row_adapter == every[None, :], values[None, :], 0), axis=1, keepdims=True)


def line_of_four(hidden, weight, down, up, row_adapter, rank_of_adapter, adapter_storage_slot):
    rows = hidden.shape[0]
    half = rows // 2
    at = lax.axis_index("dp")
    per_index = adapter_storage_slot.shape[0] // 4

    def send(v, pairs):
        return lax.ppermute(v, "tensor", pairs)

    near = [(0, 1), (1, 0), (2, 3), (3, 2)]
    middle = [(1, 2), (2, 1)]
    two = [(0, 2), (2, 0), (1, 3), (3, 1)]

    def swap(v, bit):
        return lax.ppermute(v, "dp", [(i, i ^ bit) for i in range(4)])

    places = ((adapter_storage_slot // per_index) ^ at) * per_index + adapter_storage_slot % per_index
    code = by_adapter(row_adapter, places * LANES + rank_of_adapter)

    down2, down1 = swap(down, 2), swap(down, 1)
    up2, up1 = swap(up, 2), swap(up, 1)

    cut = rows * 3 // 4
    after = rows - cut
    p0a, t = products(None, hidden, weight, [(0, 0, cut, 0, 0)], [cut])
    a1a = send(p0a, near)
    jobs = [(1, 0, half, 0, after), (1, half, half, 1, 0), (0, cut, after, 0, 0), (2, 0, rows, 2, 0)]
    p01, p1l, p2, t = products(t, hidden, weight, jobs, [after + half, half + rows // 8, rows])
    a12 = send(p01, near)
    down2, t = relay(t, down2)
    downs = (down, down1, down2, swap(down2, 1))
    v, t = add(t, p0a, a1a)
    b1a = send(v, middle)
    p1l, t = low_product(t, hidden, downs, code, p1l)
    a2l = send(p1l, near)
    v, t = add(t, p01, a12)
    b12 = send(v, middle)
    v, t = add_middle(t, p2, 0, (b1a,), [(0, half)])
    m3a = send(v, near)
    up2, t = relay(t, up2)
    ups = (up, up1, up2, swap(up2, 1))
    v, low, t = add(t, p1l, a2l, [half, rows // 8], MORE)
    b2b = send(v, middle)
    e2 = send(low, two)
    own, t = own_product(t, hidden, weight)
    m, t = add_middle(t, p2, half, (b1a, b12), [(half, cut - half), (0, after)])
    m3b = send(m, near)
    out, rest, t = up_sum(t, own, low, e2, ups, code, b12, m3a)
    return last_sum(t, out, rest, b2b, m3b)


def any_line(hidden, weight, down, up, row_adapter, rank_of_adapter, adapter_storage_slot):
    rows = hidden.shape[0]
    adapters = rank_of_adapter.shape[0]
    width = down.shape[1] * lax.axis_size("dp") // adapters
    slot = by_adapter(row_adapter, adapter_storage_slot)
    rank = by_adapter(row_adapter, rank_of_adapter)
    chosen = slot == jnp.arange(adapters, dtype=jnp.int32)[None, :]
    partial = jnp.dot(hidden, weight, preferred_element_type=F32).astype(BF16)
    base = lax.psum_scatter(partial, "tensor", scatter_dimension=1, tiled=True).astype(F32)
    downs = lax.all_gather(down, "dp", axis=1, tiled=True)
    product = jnp.dot(hidden, downs, preferred_element_type=F32)
    low = jnp.einsum("rac,ra->rc", product.reshape(rows, adapters, width), chosen.astype(F32))
    low = lax.psum(low.astype(BF16), "tensor").astype(F32)
    live = jnp.arange(width, dtype=jnp.int32)[None, :] < rank
    scaling = width / (2.0 * rank.astype(F32))
    low_rank = jnp.where(live, low * scaling, F32(0.0)).astype(BF16)
    spread = jnp.where(chosen[:, :, None], low_rank[:, None, :], jnp.zeros((), BF16)).reshape(rows, -1)
    ups = lax.all_gather(up, "dp", axis=0, tiled=True)
    return (base + jnp.dot(spread, ups, preferred_element_type=F32)).astype(BF16)


def on_device(hidden, weight, down, up, *rest):
    fits = (
        lax.axis_size("tensor") == 4
        and lax.axis_size("dp") == 4
        and down.shape[1] == LANES
        and up.shape[0] == LANES
        and rest[1].shape[0] == 8
        and hidden.shape[0] % 1024 == 0
        and hidden.shape[1] % (PIECES * LANES) == 0
        and up.shape[1] == 4 * LANES
    )
    return (line_of_four if fits else any_line)(hidden, weight, down, up, *rest)


def solution(mesh):
    return jax.shard_map(
        on_device,
        mesh=mesh,
        in_specs=(
            P(("groups", "dp"), "tensor"),
            P("tensor", None),
            P("tensor", "dp"),
            P("dp", "tensor"),
            P(("groups", "dp"), None),
            P(),
            P(),
        ),
        out_specs=P(("groups", "dp"), "tensor"),
        check_vma=False,
    )
```
